32 devices in a mesh: groups: 2 (over y), tensor: 4 (over z), batch: 4 (over x, core).
Axes of the slice: x: 2, y: 2, z: 4, core: 2. Of those that a mesh axis runs over, the one named last changes fastest.
Arguments:
- latent: bfloat16 [8, 64, 5120], P(('groups', 'batch'), None, 'tensor'), parts along dimension 0, may hold values from -6 to 6
- mod_table: bfloat16 [2, 8, 3, 5120], P(None, None, None, 'tensor'), may hold values from -3 to 3
- skip_layer: int32 [8], P(('groups', 'batch')), parts along dimension 0, may hold values from 0 to 1
- step_index: int32 [8], P(('groups', 'batch')), parts along dimension 0, may hold values from 0 to 7
- up_weight: bfloat16 [2, 5120, 7680], P(None, None, 'tensor'), may hold values from -0.078125 to 0.078125
- down_weight: bfloat16 [2, 7680, 5120], P(None, 'tensor'), may hold values from -0.09375 to 0.09375
- up_in: bfloat16 [2, 5120, 64], P(None, ('tensor', 'batch')), may hold values from -0.75 to 0.75
- up_out: bfloat16 [2, 64, 7680], P(None, None, 'tensor'), may hold values from -0.078125 to 0.078125
- down_in: bfloat16 [2, 7680, 64], P(None, 'tensor'), may hold values from -0.75 to 0.75
- down_out: bfloat16 [2, 64, 5120], P(None, None, ('tensor', 'batch')), may hold values from -0.0625 to 0.0625
Outputs:
- guided: bfloat16 [8, 64, 5120], P(('groups', 'batch'), None, 'tensor'), parts along dimension 0
The draws below stay inside these ranges and needn't reach their ends.
There are 2 independent parts, one for each index of `groups`. The reference program is written for one: setup_inputs(seed, part) draws one part's arguments, and reference() takes and returns one part's arrays. A program takes and returns all parts, laid end to end along the dimension named above; an argument that names none is the same for every part. Nothing has to cross between parts.
All inputs are finite; a program needn't handle non-finite values.
Results may differ from the reference program's by a relative error of at most 0.0082.
Values may be sent and summed in bfloat16 or wider, within the bound.
A program may use at most 320 MiB of HBM per device.

```python
import jax
import jax.numpy as jnp
from jax import lax

D = 5120
FFW = 7680
R = 64
L = 2
STEPS = 8
T_SIZE = 64
CLIPS = 4


def with_ends(array, key, least, top_value):
    dims = array.shape
    place = [jax.random.randint(jax.random.fold_in(key, axis), (), 0, dims[axis]) for axis in range(len(dims))]
    array = array.at[tuple(place)].set(least)
    longest = dims.index(max(dims))
    place[longest] = (place[longest] + 1) % dims[longest]
    return array.at[tuple(place)].set(top_value)


def strengthened(array, key, source, target, blocks, factor):
    owner, partner = [(jnp.arange(array.shape[position]) // (array.shape[position] // blocks)).reshape([-1 if axis == position else 1 for axis in range(array.ndim)]) for position in (source, target)]
    chosen = jax.random.permutation(key, blocks)[partner]
    strong = (owner == chosen) | (owner == (partner + blocks // 2) % blocks)
    return jnp.where(strong, factor * array, array)


def shard_levels(stream_key, dims, cuts, least, top_value):
    def one(position, shards_of):
        heights = jax.random.uniform(jax.random.fold_in(jax.random.fold_in(stream_key, 6), position), (shards_of,), jnp.float32, least / len(cuts), top_value / len(cuts))
        return jnp.repeat(jnp.exp(heights), dims[position] // shards_of).reshape((-1,) + (1,) * (len(dims) - position - 1))

    loudness = one(*cuts[0])
    for cut in cuts[1:]:
        loudness = loudness * one(*cut)
    return loudness


def noise(rng, extent, deviation, reach, pieces=(), held_as=jnp.bfloat16):
    drawn = jax.random.normal(rng, extent, jnp.float32) * deviation
    if len(pieces) > 0:
        drawn = shard_levels(rng, extent, pieces, -0.22, 0.18) * drawn
    return jnp.clip(drawn, min=-reach, max=reach).astype(held_as)


def heavy_noise(stream_key, shape, width, limit, pieces, heavy, held_as=jnp.bfloat16):
    entries = width * jax.random.normal(stream_key, shape, jnp.float32)
    if pieces:
        entries = entries * shard_levels(stream_key, shape, pieces, -0.22, 0.18)
    return jnp.clip(strengthened(entries, jax.random.fold_in(stream_key, 3), *heavy), -limit, limit).astype(held_as)


def setup_inputs(seed: int = 0, part: int = 0) -> dict:
    splits = jax.random.split(jax.random.key(seed), 11)
    own_keys = jax.random.split(jax.random.fold_in(splits[10], part), 11)
    return {
        "latent": noise(own_keys[0], (CLIPS, T_SIZE, D), 1.0, 6.0, ((0, 4), (2, 4))),
        "mod_table": noise(splits[1], (L, STEPS, 3, D), 0.5, 3.0, ((3, 4),)),
        "skip_layer": with_ends(jax.random.randint(own_keys[2], (CLIPS,), 0, L), jax.random.fold_in(own_keys[2], 1), 0, L - 1).astype(jnp.int32),
        "step_index": with_ends(jax.random.randint(own_keys[3], (CLIPS,), 0, STEPS), jax.random.fold_in(own_keys[3], 1), 0, STEPS - 1).astype(jnp.int32),
        "up_weight": noise(splits[4], (L, D, FFW), D ** -0.5, 0.078125, ((2, 4),)),
        "down_weight": heavy_noise(splits[5], (L, FFW, D), FFW ** -0.5, 0.09375, ((1, 4),), (1, 2, 4, 2.0)),
        "up_in": noise(splits[6], (L, D, R), R ** -0.5, 0.75, ((1, 16),)),
        "up_out": noise(splits[7], (L, R, FFW), D ** -0.5, 0.078125, ((2, 4),)),
        "down_in": noise(splits[8], (L, FFW, R), R ** -0.5, 0.75, ((1, 4),)),
        "down_out": noise(splits[9], (L, R, D), FFW ** -0.5, 0.0625, ((2, 16),)),
    }


guide_weight = 1.0

def modulate(rows, mod):
    values = rows.astype(jnp.float32)
    center = values - lax.optimization_barrier(jnp.mean(values, axis=-1, keepdims=True))
    spread = lax.optimization_barrier(jnp.mean(center * center, axis=-1, keepdims=True))
    normed = center * lax.rsqrt(spread + 1e-06)
    return (normed * (1.0 + mod[1]) + mod[0]).astype(jnp.bfloat16)

def feed(rows, mod, w_up, w_down):
    hidden = jnp.dot(modulate(rows, mod), w_up, preferred_element_type=jnp.float32)
    active = jax.nn.gelu(hidden, approximate=True).astype(jnp.bfloat16)
    return jnp.dot(active, w_down, preferred_element_type=jnp.float32)

def reference(latent, mod_table, skip_layer, step_index, up_weight, down_weight, up_in, up_out, down_in, down_out):
    ups = [(up_weight[level].astype(jnp.float32) + jnp.dot(up_in[level], up_out[level], preferred_element_type=jnp.float32)).astype(jnp.bfloat16) for level in range(L)]
    downs = [(down_weight[level].astype(jnp.float32) + jnp.dot(down_in[level], down_out[level], preferred_element_type=jnp.float32)).astype(jnp.bfloat16) for level in range(L)]
    results = []
    for clip in range(CLIPS):
        tokens = latent[clip]
        mods = mod_table[:, step_index[clip]].astype(jnp.float32)
        first = (tokens.astype(jnp.float32) + mods[0, 2] * feed(tokens, mods[0], ups[0], downs[0])).astype(jnp.bfloat16)
        full = first.astype(jnp.float32) + mods[1, 2] * feed(first, mods[1], ups[1], downs[1])
        other = tokens.astype(jnp.float32) + mods[1, 2] * feed(tokens, mods[1], ups[1], downs[1])
        skipped = jnp.where(skip_layer[clip] == 0, other, first.astype(jnp.float32))
        results.append((full + guide_weight * (full - skipped)).astype(jnp.bfloat16))
    return jnp.stack(results)
```

```python
import jax
import jax.numpy as jnp
from jax import lax
from jax.sharding import PartitionSpec as P

guide_weight = 1.0


def modulate(rows, mod):
    values = rows.astype(jnp.float32)
    center = values - jnp.mean(values, axis=-1, keepdims=True)
    spread = jnp.mean(center * center, axis=-1, keepdims=True)
    normed = center * lax.rsqrt(spread + 1e-06)
    return (normed * (1.0 + mod[1]) + mod[0]).astype(jnp.bfloat16)


def dot32(a, b):
    return jnp.dot(a, b, preferred_element_type=jnp.float32)


def own_columns(array, width):
    start = lax.axis_index("tensor") * width
    return lax.dynamic_slice_in_dim(array, start, width, axis=1)


def hidden_of(rows, mod, w_up, a_own, up_out):
    normed = modulate(rows, mod)
    low = lax.psum(dot32(own_columns(normed, a_own.shape[0]), a_own), "tensor")
    return dot32(normed, w_up) + dot32(low.astype(jnp.bfloat16), up_out)


def project_down(active, w_down, down_in, d_own):
    low = lax.psum(dot32(active, down_in), "tensor")
    total = lax.psum_scatter(dot32(active, w_down), "tensor", scatter_dimension=1, tiled=True)
    return total + dot32(low.astype(jnp.bfloat16), d_own)


def gelu(x):
    return jax.nn.gelu(x, approximate=True)


def per_device(
    latent,
    mod_table,
    skip_layer,
    step_index,
    up_weight,
    down_weight,
    up_in,
    up_out,
    down_in,
    down_out,
):
    tokens = latent[0]
    keep = (skip_layer[0] == 0).astype(jnp.float32)
    mods = lax.dynamic_index_in_dim(mod_table, step_index[0], axis=1, keepdims=False)
    mods_local = mods.astype(jnp.float32)
    a_own = lax.all_gather(up_in, "batch", axis=1, tiled=True)
    d_own = lax.all_gather(down_out, "batch", axis=2, tiled=True)
    tokens_full = lax.all_gather(tokens, "tensor", axis=1, tiled=True)
    mods_full = lax.all_gather(mods[:, :2], "tensor", axis=2, tiled=True).astype(jnp.float32)
    hidden = hidden_of(tokens_full, mods_full[0], up_weight[0], a_own[0], up_out[0])
    active = gelu(hidden).astype(jnp.bfloat16)
    first_sum = project_down(active, down_weight[0], down_in[0], d_own[0])
    token_value = tokens.astype(jnp.float32)
    first = (token_value + mods_local[0, 2] * first_sum).astype(jnp.bfloat16)
    first_full = lax.all_gather(first, "tensor", axis=1, tiled=True)
    count = tokens.shape[0]
    stacked = jnp.concatenate([first_full, tokens_full], axis=0)
    hidden = gelu(hidden_of(stacked, mods_full[1], up_weight[1], a_own[1], up_out[1]))
    active = ((1.0 + guide_weight) * hidden[:count] - (guide_weight * keep) * hidden[count:]).astype(jnp.bfloat16)
    summed = project_down(active, down_weight[1], down_in[1], d_own[1])
    first_value = first.astype(jnp.float32)
    start = first_value + guide_weight * keep * (first_value - token_value)
    return (start + mods_local[1, 2] * summed).astype(jnp.bfloat16)[None]


def solution(mesh):
    placed = (
        P(("groups", "batch"), None, "tensor"),
        P(None, None, None, "tensor"),
        P(("groups", "batch")),
        P(("groups", "batch")),
        P(None, None, "tensor"),
        P(None, "tensor", None),
        P(None, ("tensor", "batch"), None),
        P(None, None, "tensor"),
        P(None, "tensor", None),
        P(None, None, ("tensor", "batch")),
    )
    return jax.shard_map(
        per_device,
        mesh=mesh,
        in_specs=placed,
        out_specs=P(("groups", "batch"), None, "tensor"),
        check_vma=False,
    )
```

```python
import functools

import jax
import jax.numpy as jnp
from jax import lax
from jax.experimental import pallas as pl
from jax.experimental.pallas import tpu as pltpu
from jax.sharding import PartitionSpec as P

guide_weight = 1.0


def modulate(rows, mod):
    values = rows.astype(jnp.float32)
    center = values - jnp.mean(values, axis=-1, keepdims=True)
    spread = jnp.mean(center * center, axis=-1, keepdims=True)
    normed = center * lax.rsqrt(spread + 1e-06)
    return (normed * (1.0 + mod[1]) + mod[0]).astype(jnp.bfloat16)


def dot32(a, b):
    return jnp.dot(a, b, preferred_element_type=jnp.float32)


def own_columns(array, width):
    start = lax.axis_index("tensor") * width
    return lax.dynamic_slice_in_dim(array, start, width, axis=1)


def hidden_of(rows, mod, w_up, a_own, up_out):
    normed = modulate(rows, mod)
    low = lax.psum(dot32(own_columns(normed, a_own.shape[0]), a_own), "tensor")
    return dot32(normed, w_up) + dot32(low.astype(jnp.bfloat16), up_out)


def project_down(active, w_down, down_in, d_own):
    low = lax.psum(dot32(active, down_in), "tensor")
    total = lax.psum_scatter(dot32(active, w_down), "tensor", scatter_dimension=1, tiled=True)
    return total + dot32(low.astype(jnp.bfloat16), d_own)


def gelu(x):
    return jax.nn.gelu(x, approximate=True)


def per_device(
    latent,
    mod_table,
    skip_layer,
    step_index,
    up_weight,
    down_weight,
    up_in,
    up_out,
    down_in,
    down_out,
):
    tokens = latent[0]
    keep = (skip_layer[0] == 0).astype(jnp.float32)
    mods = lax.dynamic_index_in_dim(mod_table, step_index[0], axis=1, keepdims=False)
    mods_local = mods.astype(jnp.float32)
    a_own = lax.all_gather(up_in, "batch", axis=1, tiled=True)
    d_own = lax.all_gather(down_out, "batch", axis=2, tiled=True)
    tokens_full = lax.all_gather(tokens, "tensor", axis=1, tiled=True)
    mods_full = lax.all_gather(mods[:, :2], "tensor", axis=2, tiled=True).astype(jnp.float32)
    hidden = hidden_of(tokens_full, mods_full[0], up_weight[0], a_own[0], up_out[0])
    active = gelu(hidden).astype(jnp.bfloat16)
    first_sum = project_down(active, down_weight[0], down_in[0], d_own[0])
    token_value = tokens.astype(jnp.float32)
    first = (token_value + mods_local[0, 2] * first_sum).astype(jnp.bfloat16)
    first_full = lax.all_gather(first, "tensor", axis=1, tiled=True)
    count = tokens.shape[0]
    stacked = jnp.concatenate([first_full, tokens_full], axis=0)
    hidden = gelu(hidden_of(stacked, mods_full[1], up_weight[1], a_own[1], up_out[1]))
    active = ((1.0 + guide_weight) * hidden[:count] - (guide_weight * keep) * hidden[count:]).astype(jnp.bfloat16)
    summed = project_down(active, down_weight[1], down_in[1], d_own[1])
    first_value = first.astype(jnp.float32)
    start = first_value + guide_weight * keep * (first_value - token_value)
    return (start + mods_local[1, 2] * summed).astype(jnp.bfloat16)[None]


T_NAME = "tensor"
B_NAME = "batch"
LANES = 128


def matmul_tiles(width, tile, body):
    whole = width // tile

    @pl.loop(0, whole)
    def _(i):
        body(pl.multiple_of(i * tile, tile), tile)

    if width % tile:
        body(whole * tile, width % tile)


def moments(values):
    mean = jnp.mean(values, axis=-1, keepdims=True)
    center = values - mean
    return mean, jnp.sum(center * center, axis=-1, keepdims=True)


def pack_moments(values):
    mean, square = moments(values)
    count = values.shape[0]
    lane = lax.broadcasted_iota(jnp.int32, (count, LANES), 1)
    both = jnp.where(lane == 0, mean, jnp.where(lane == 1, square, 0.0))
    if count < LANES:
        both = jnp.concatenate([both, jnp.zeros((LANES - count, LANES), jnp.float32)], axis=0)
    return both.T[:8]


def unpack_moments(packed, count):
    whole = jnp.concatenate([packed, jnp.zeros((LANES - 8, LANES), jnp.float32)], axis=0).T
    return whole[:count, 0:1], whole[:count, 1:2]


def window_kernel(
    n, nb,
    keep_ref, lat_ref, mod_ref, gate_ref, ad_ref, uo_ref, di_ref, uw, dw,
    out_ref,
    rows_all, mod_all, stat_all, low_all, back_all, ad_all, sums_in, sums_out,
    normed, act, hid, own, stat_mine, low_mine, back_mine,
    up_buf, down_buf,
    up_sem, down_sem,
    rows_s, rows_r, mod_s, mod_r, stat_s, stat_r, low_s, low_r, back_s, back_r, ad_s, ad_r, sum_s, sum_r,
):
    me = lax.axis_index(T_NAME)
    mb = lax.axis_index(B_NAME)
    count, width = lat_ref.shape
    units = uo_ref.shape[1]
    part = ad_ref.shape[1]
    up_slots = up_buf.shape[0]
    lane_rows = width // LANES
    keep = keep_ref[0]
    f32, bf16 = jnp.float32, jnp.bfloat16

    def up_copy(level, step):
        chunk = level * n + step
        block = lax.rem(me + n - step, n)
        rows = pl.ds(pl.multiple_of(block * width, LANES), width)
        return pltpu.make_async_copy(uw.at[level, rows, :], up_buf.at[chunk % up_slots], up_sem.at[chunk])

    def down_copy(level, step):
        block = lax.rem(me + 1 + step, n)
        columns = pl.ds(pl.multiple_of(block * width, LANES), width)
        return pltpu.make_async_copy(dw.at[level, :, columns], down_buf.at[step], down_sem.at[level * n + step])

    for step in range(n):
        up_copy(0, step).start()
    for step in range(n):
        down_copy(0, step).start()
    for step in range(up_slots - n):
        up_copy(1, step).start()

    sent = []

    def send(src, dst, s, r, where):
        copy = pltpu.make_async_remote_copy(
            src_ref=src, dst_ref=dst, send_sem=s, recv_sem=r,
            device_id=where, device_id_type=pl.DeviceIdType.MESH)
        copy.start()
        sent.append(copy)

    def arrive(buf, r):
        pltpu.make_async_remote_copy(
            src_ref=buf, dst_ref=buf, send_sem=r, recv_sem=r,
            device_id={T_NAME: lax.rem(me + 1, n)}, device_id_type=pl.DeviceIdType.MESH).wait_recv()

    def to_peers(src, dst, s, r):
        for step in range(1, n):
            send(src, dst, s.at[step], r.at[me], {T_NAME: lax.rem(me + step, n)})

    def from_peers(buf, r):
        for step in range(1, n):
            block = lax.rem(me + n - step, n)
            arrive(buf.at[block], r.at[block])

    stat_mine[0] = pack_moments(lat_ref[...].astype(f32))
    barrier = pltpu.get_barrier_semaphore()
    for step in range(1, n):
        pl.semaphore_signal(barrier, inc=1, device_id={T_NAME: lax.rem(me + step, n)}, device_id_type=pl.DeviceIdType.MESH)
    for step in range(1, nb):
        pl.semaphore_signal(barrier, inc=1, device_id={B_NAME: lax.rem(mb + step, nb)}, device_id_type=pl.DeviceIdType.MESH)
    pl.semaphore_wait(barrier, n - 1 + nb - 1)

    to_peers(stat_mine.at[0], stat_all.at[0, me], stat_s.at[0], stat_r.at[0])
    to_peers(mod_ref, mod_all.at[me], mod_s, mod_r)
    to_peers(lat_ref, rows_all.at[0, me], rows_s.at[0], rows_r.at[0])
    spot = pl.ds(pl.multiple_of(mb * part, 16), part)
    for level in range(2):
        for step in range(1, nb):
            send(ad_ref.at[level], ad_all.at[level, spot, :], ad_s.at[level, step], ad_r.at[level, mb], {B_NAME: lax.rem(mb + step, nb)})
    mod_all[me] = mod_ref[...]
    ad_all[:, spot, :] = ad_ref[...]
    stat_all[0, me] = stat_mine[0]
    rows_all[0, me] = lat_ref[...]

    def wait_ad(level):
        for step in range(1, nb):
            other = lax.rem(mb + step, nb)
            there = pl.ds(pl.multiple_of(other * part, 16), part)
            arrive(ad_all.at[level, there, :], ad_r.at[level, other])

    def statistics(kind):
        parts = [unpack_moments(stat_all[kind, b], count) for b in range(n)]
        mean = sum(p[0] for p in parts) * (1.0 / n)
        square = sum(p[1] + width * (p[0] - mean) * (p[0] - mean) for p in parts)
        return mean, lax.rsqrt(square * (1.0 / (n * width)) + 1e-06)

    def mod_row(block, row):
        return jnp.concatenate([mod_all[block, row * lane_rows + j : row * lane_rows + j + 1, :] for j in range(lane_rows)], axis=1)

    def apply(kind, level, block, stats):
        values = rows_all[kind, block].astype(f32)
        return ((values - stats[0]) * stats[1] * (1.0 + mod_row(block, 2 * level + 1)) + mod_row(block, 2 * level)).astype(bf16)

    def up_step(slot, target, init):
        def body(start, size):
            columns = pl.ds(start, size)
            value = jnp.dot(normed[...], up_buf[slot, :, columns], preferred_element_type=f32)
            if init:
                hid[target, :, columns] = value
            else:
                hid[target, :, columns] += value

        matmul_tiles(units, 512, body)

    def add_low(target, low):
        def body(start, size):
            columns = pl.ds(start, size)
            hid[target, :, columns] += jnp.dot(low, uo_ref[:, columns], preferred_element_type=f32)

        matmul_tiles(units, 512, body)

    half = lax.broadcasted_iota(jnp.int32, (count, LANES), 1) < LANES // 2

    def low_sum(kind):
        return sum(low_all[kind, b] for b in range(n))

    def back_projection(level):
        value = jnp.dot(act[...], di_ref[...], preferred_element_type=f32)
        mine = half if level == 1 else jnp.logical_not(half)
        back_mine[level] = jnp.where(mine, value, 0.0)
        back_all[level, me] = back_mine[level]
        to_peers(back_mine.at[level], back_all.at[level, me], back_s.at[level], back_r.at[level])

    def down_steps(level):
        for step in range(n):
            down_copy(level, step).wait()

            def body(start, size):
                columns = pl.ds(start, size)
                value = jnp.dot(act[...], down_buf[step, :, columns], preferred_element_type=f32)
                if step < n - 1:
                    sums_out[level, step, :, columns] = value.astype(bf16)
                else:
                    own[:, columns] = value

            matmul_tiles(width, 256, body)
            if step < n - 1:
                send(sums_out.at[level, step], sums_in.at[level, me], sum_s.at[level, step], sum_r.at[level, me], {T_NAME: lax.rem(me + 1 + step, n)})
            if level == 0:
                down_copy(1, step).start()

    def settle(level):
        from_peers(back_all.at[level], back_r.at[level])
        low = sum(back_all[level, b] for b in range(n)).astype(bf16)
        total = own[...] + lax.dot_general(low, ad_all[level], (((1,), (1,)), ((), ())), preferred_element_type=f32)
        from_peers(sums_in.at[level], sum_r.at[level])
        for step in range(1, n):
            total = total + sums_in[level, lax.rem(me + step, n)].astype(f32)
        return total

    from_peers(stat_all.at[0], stat_r.at[0])
    from_peers(mod_all, mod_r)
    lat_stats = statistics(0)
    wait_ad(0)
    low0 = jnp.dot(apply(0, 0, me, lat_stats), ad_all[0], preferred_element_type=f32)
    wait_ad(1)
    low1 = jnp.dot(apply(0, 1, me, lat_stats), ad_all[1], preferred_element_type=f32)
    low_mine[0] = jnp.where(half, low0, low1)
    low_all[0, me] = low_mine[0]
    to_peers(low_mine.at[0], low_all.at[0, me], low_s.at[0], low_r.at[0])
    for step in range(n):
        block = lax.rem(me + n - step, n)
        if step:
            arrive(rows_all.at[0, block], rows_r.at[0, block])
        normed[...] = apply(0, 0, block, lat_stats)
        up_copy(0, step).wait()
        up_step(step, 0, step == 0)
        later = up_slots - n + step
        if later < n:
            up_copy(1, later).start()
    from_peers(low_all.at[0], low_r.at[0])
    add_low(0, jnp.where(half, low_sum(0), 0.0).astype(bf16))
    act[...] = jax.nn.gelu(hid[0], approximate=True).astype(bf16)
    back_projection(0)
    down_steps(0)
    for step in range(n):
        block = lax.rem(me + n - step, n)
        normed[...] = apply(0, 1, block, lat_stats)
        up_copy(1, step).wait()
        up_step((n + step) % up_slots, 1, step == 0)
    add_low(1, jnp.where(half, 0.0, low_sum(0)).astype(bf16))
    hid[1] = jax.nn.gelu(hid[1], approximate=True)
    first = (lat_ref[...].astype(f32) + gate_ref[0:1, :] * settle(0)).astype(bf16)
    rows_all[1, me] = first
    stat_mine[1] = pack_moments(first.astype(f32))
    to_peers(stat_mine.at[1], stat_all.at[1, me], stat_s.at[1], stat_r.at[1])
    to_peers(rows_all.at[1, me], rows_all.at[1, me], rows_s.at[1], rows_r.at[1])
    stat_all[1, me] = stat_mine[1]
    from_peers(stat_all.at[1], stat_r.at[1])
    stats = statistics(1)
    low = jnp.dot(apply(1, 1, me, stats), ad_all[1], preferred_element_type=f32)
    low_mine[1] = jnp.where(half, 0.0, low)
    low_all[1, me] = low_mine[1]
    to_peers(low_mine.at[1], low_all.at[1, me], low_s.at[1], low_r.at[1])
    for step in range(n):
        block = lax.rem(me + n - step, n)
        if step:
            arrive(rows_all.at[1, block], rows_r.at[1, block])
        normed[...] = apply(1, 1, block, stats)
        up_step((n + step) % up_slots, 0, step == 0)
    from_peers(low_all.at[1], low_r.at[1])
    add_low(0, low_sum(1).astype(bf16))
    active = jax.nn.gelu(hid[0], approximate=True)
    act[...] = ((1.0 + guide_weight) * active - (guide_weight * keep) * hid[1]).astype(bf16)
    back_projection(1)
    down_steps(1)
    total = settle(1)
    first_value = rows_all[1, me].astype(f32)
    start = first_value + guide_weight * keep * (first_value - lat_ref[...].astype(f32))
    out_ref[...] = (start + gate_ref[1:2, :] * total).astype(out_ref.dtype)
    for copy in sent:
        copy.wait_send()


def per_device_fused(n, nb, latent, mod_table, skip_layer, step_index, up_weight, down_weight, up_in, up_out, down_in, down_out):
    f32, bf16 = jnp.float32, jnp.bfloat16
    tokens = latent[0]
    count, width = tokens.shape
    units = up_weight.shape[2]
    keep = (skip_layer == 0).astype(f32)
    mods = lax.dynamic_index_in_dim(mod_table, step_index[0], axis=1, keepdims=False).astype(f32)
    lane_rows = 4 * width // LANES
    mod_packed = mods[:, :2].reshape(lane_rows, LANES)
    gates = mods[:, 2]
    turned = jnp.swapaxes(down_out, 1, 2)
    ad = jnp.stack([jnp.concatenate([up_in[0], turned[0]], axis=1), jnp.concatenate([turned[1], up_in[1]], axis=1)])
    di = jnp.concatenate([down_in[1], down_in[0]], axis=1)
    uo = up_out.reshape(LANES, units)
    up_slots = n + 2
    vmem = pl.BlockSpec(memory_space=pltpu.VMEM)
    hbm = pl.BlockSpec(memory_space=pl.ANY)
    dma = pltpu.SemaphoreType.DMA
    part = ad.shape[1]
    return pl.pallas_call(
        functools.partial(window_kernel, n, nb),
        out_shape=jax.ShapeDtypeStruct((count, width), bf16),
        in_specs=[pl.BlockSpec(memory_space=pltpu.SMEM)] + [vmem] * 6 + [hbm] * 2,
        out_specs=vmem,
        scratch_shapes=[
            pltpu.VMEM((2, n, count, width), bf16),
            pltpu.VMEM((n, lane_rows, LANES), f32),
            pltpu.VMEM((2, n, 8, LANES), f32),
            pltpu.VMEM((2, n, count, LANES), f32),
            pltpu.VMEM((2, n, count, LANES), f32),
            pltpu.VMEM((2, part * nb, LANES), bf16),
            pltpu.VMEM((2, n, count, width), bf16),
            pltpu.VMEM((2, n - 1, count, width), bf16),
            pltpu.VMEM((count, width), bf16),
            pltpu.VMEM((count, units), bf16),
            pltpu.VMEM((2, count, units), f32),
            pltpu.VMEM((count, width), f32),
            pltpu.VMEM((2, 8, LANES), f32),
            pltpu.VMEM((2, count, LANES), f32),
            pltpu.VMEM((2, count, LANES), f32),
            pltpu.VMEM((up_slots, width, units), bf16),
            pltpu.VMEM((n, units, width), bf16),
            dma((2 * n,)), dma((2 * n,)),
            dma((2, n)), dma((2, n)),
            dma((n,)), dma((n,)),
            dma((2, n)), dma((2, n)),
            dma((2, n)), dma((2, n)),
            dma((2, n)), dma((2, n)),
            dma((2, nb)), dma((2, nb)),
            dma((2, n)), dma((2, n)),
        ],
        compiler_params=pltpu.CompilerParams(collective_id=0, has_side_effects=True, vmem_limit_bytes=63 * 2**20),
        cost_estimate=pl.CostEstimate(flops=8 * 10**9, bytes_accessed=80 * 10**6, transcendentals=400000),
    )(keep, tokens, mod_packed, gates, ad, uo, di, up_weight, down_weight)[None]


def solution(mesh):
    placed = (
        P(("groups", "batch"), None, "tensor"),
        P(None, None, None, "tensor"),
        P(("groups", "batch")),
        P(("groups", "batch")),
        P(None, None, "tensor"),
        P(None, "tensor", None),
        P(None, ("tensor", "batch"), None),
        P(None, None, "tensor"),
        P(None, "tensor", None),
        P(None, None, ("tensor", "batch")),
    )
    n, nb = mesh.shape["tensor"], mesh.shape["batch"]

    def one_device(*arrays):
        latent, up_weight, up_out = arrays[0], arrays[4], arrays[7]
        count, width = latent.shape[1:]
        units, rank = up_weight.shape[2], up_out.shape[1]
        aligned = width % LANES == 0 and units % LANES == 0 and 2 * rank == LANES
        small = n * width * units * 2 <= 20 * 2**20 and n > 2 and nb > 1
        if aligned and small and count % 16 == 0 and count <= LANES:
            return per_device_fused(n, nb, *arrays)
        return per_device(*arrays)

    return jax.shard_map(
        one_device,
        mesh=mesh,
        in_specs=placed,
        out_specs=P(("groups", "batch"), None, "tensor"),
        check_vma=False,
    )
```

```python
import functools

import jax
import jax.numpy as jnp
from jax import lax
from jax.experimental import pallas as pl
from jax.experimental.pallas import tpu as pltpu
from jax.sharding import PartitionSpec as P

guide_weight = 1.0


def modulate(rows, mod):
    values = rows.astype(jnp.float32)
    center = values - jnp.mean(values, axis=-1, keepdims=True)
    spread = jnp.mean(center * center, axis=-1, keepdims=True)
    normed = center * lax.rsqrt(spread + 1e-06)
    return (normed * (1.0 + mod[1]) + mod[0]).astype(jnp.bfloat16)


def dot32(a, b):
    return jnp.dot(a, b, preferred_element_type=jnp.float32)


def own_columns(array, width):
    start = lax.axis_index("tensor") * width
    return lax.dynamic_slice_in_dim(array, start, width, axis=1)


def hidden_of(rows, mod, w_up, a_own, up_out):
    normed = modulate(rows, mod)
    low = lax.psum(dot32(own_columns(normed, a_own.shape[0]), a_own), "tensor")
    return dot32(normed, w_up) + dot32(low.astype(jnp.bfloat16), up_out)


def project_down(active, w_down, down_in, d_own):
    low = lax.psum(dot32(active, down_in), "tensor")
    total = lax.psum_scatter(dot32(active, w_down), "tensor", scatter_dimension=1, tiled=True)
    return total + dot32(low.astype(jnp.bfloat16), d_own)


def gelu(x):
    return jax.nn.gelu(x, approximate=True)


def per_device(
    latent,
    mod_table,
    skip_layer,
    step_index,
    up_weight,
    down_weight,
    up_in,
    up_out,
    down_in,
    down_out,
):
    tokens = latent[0]
    keep = (skip_layer[0] == 0).astype(jnp.float32)
    mods = lax.dynamic_index_in_dim(mod_table, step_index[0], axis=1, keepdims=False)
    mods_local = mods.astype(jnp.float32)
    a_own = lax.all_gather(up_in, "batch", axis=1, tiled=True)
    d_own = lax.all_gather(down_out, "batch", axis=2, tiled=True)
    tokens_full = lax.all_gather(tokens, "tensor", axis=1, tiled=True)
    mods_full = lax.all_gather(mods[:, :2], "tensor", axis=2, tiled=True).astype(jnp.float32)
    hidden = hidden_of(tokens_full, mods_full[0], up_weight[0], a_own[0], up_out[0])
    active = gelu(hidden).astype(jnp.bfloat16)
    first_sum = project_down(active, down_weight[0], down_in[0], d_own[0])
    token_value = tokens.astype(jnp.float32)
    first = (token_value + mods_local[0, 2] * first_sum).astype(jnp.bfloat16)
    first_full = lax.all_gather(first, "tensor", axis=1, tiled=True)
    count = tokens.shape[0]
    stacked = jnp.concatenate([first_full, tokens_full], axis=0)
    hidden = gelu(hidden_of(stacked, mods_full[1], up_weight[1], a_own[1], up_out[1]))
    active = ((1.0 + guide_weight) * hidden[:count] - (guide_weight * keep) * hidden[count:]).astype(jnp.bfloat16)
    summed = project_down(active, down_weight[1], down_in[1], d_own[1])
    first_value = first.astype(jnp.float32)
    start = first_value + guide_weight * keep * (first_value - token_value)
    return (start + mods_local[1, 2] * summed).astype(jnp.bfloat16)[None]


T_NAME = "tensor"
B_NAME = "batch"
LANES = 128


def matmul_tiles(width, tile, body):
    whole = width // tile

    @pl.loop(0, whole)
    def _(i):
        body(pl.multiple_of(i * tile, tile), tile)

    if width % tile:
        body(whole * tile, width % tile)


def moments(values):
    mean = jnp.mean(values, axis=-1, keepdims=True)
    center = values - mean
    return mean, jnp.sum(center * center, axis=-1, keepdims=True)


def pack_moments(values):
    mean, square = moments(values)
    count = values.shape[0]
    lane = lax.broadcasted_iota(jnp.int32, (count, LANES), 1)
    both = jnp.where(lane == 0, mean, jnp.where(lane == 1, square, 0.0))
    if count < LANES:
        both = jnp.concatenate([both, jnp.zeros((LANES - count, LANES), jnp.float32)], axis=0)
    return both.T[:8]


def unpack_moments(packed, count):
    whole = jnp.concatenate([packed, jnp.zeros((LANES - 8, LANES), jnp.float32)], axis=0).T
    return whole[:count, 0:1], whole[:count, 1:2]


def window_kernel(
    n, nb,
    keep_ref, step_ref, lat_ref, table_ref, ad_ref, uo_ref, di_ref, uw, dw,
    out_ref,
    rows_all, mod_mine, gates, mod_all, stat_all, low_all, back_all, ad_all, sums_in, sums_out,
    normed, act, hid, own, stat_mine, low_mine, back_mine,
    up_buf, down_buf,
    up_sem, down_sem,
    rows_s, rows_r, mod_s, mod_r, stat_s, stat_r, low_s, low_r, back_s, back_r, ad_s, ad_r, sum_s, sum_r, left_s,
):
    me = lax.axis_index(T_NAME)
    mb = lax.axis_index(B_NAME)
    count, width = lat_ref.shape
    units = uo_ref.shape[1]
    part = ad_ref.shape[1]
    up_slots = up_buf.shape[0]
    lane_rows = width // LANES
    keep = keep_ref[0]
    f32, bf16 = jnp.float32, jnp.bfloat16

    def up_slot(level, block):
        return lax.rem(level * n + block, up_slots)

    def up_copy(level, block):
        rows = pl.ds(pl.multiple_of(block * width, LANES), width)
        return pltpu.make_async_copy(uw.at[level, rows, :], up_buf.at[up_slot(level, block)], up_sem.at[level * n + block])

    def down_copy(level, step):
        block = lax.rem(me + 1 + step, n)
        columns = pl.ds(pl.multiple_of(block * width, LANES), width)
        return pltpu.make_async_copy(dw.at[level, :, columns], down_buf.at[step], down_sem.at[level * n + step])

    for step in range(n):
        up_copy(0, lax.rem(me + step, n)).start()
    for step in range(n):
        down_copy(0, step).start()
    for step in range(up_slots - n):
        up_copy(1, step).start()

    sent = []

    def send(src, dst, s, r, where):
        copy = pltpu.make_async_remote_copy(
            src_ref=src, dst_ref=dst, send_sem=s, recv_sem=r,
            device_id=where, device_id_type=pl.DeviceIdType.MESH)
        copy.start()
        sent.append(copy)

    def arrive(buf, r):
        pltpu.make_async_remote_copy(
            src_ref=buf, dst_ref=buf, send_sem=r, recv_sem=r,
            device_id={T_NAME: lax.rem(me + 1, n)}, device_id_type=pl.DeviceIdType.MESH).wait_recv()

    def relay(kind, hop, right):
        block, target = (me - hop, me + 1) if right else (me + hop, me - 1)
        return pltpu.make_async_remote_copy(
            src_ref=rows_all.at[kind, block], dst_ref=rows_all.at[kind, block],
            send_sem=rows_s.at[kind, block], recv_sem=rows_r.at[kind, block],
            device_id={T_NAME: target}, device_id_type=pl.DeviceIdType.MESH)

    def comes(hop, right):
        return me >= hop if right else me + hop < n

    def goes(hop, right):
        return jnp.logical_and(me >= hop, me + 1 < n) if right else jnp.logical_and(me + hop < n, me > 0)

    def own_rows(kind):
        @pl.when(me + 1 < n)
        def _():
            relay(kind, 0, True).start()

        @pl.when(me > 0)
        def _():
            pltpu.make_async_remote_copy(
                src_ref=rows_all.at[kind, me], dst_ref=rows_all.at[kind, me],
                send_sem=left_s.at[kind], recv_sem=rows_r.at[kind, me],
                device_id={T_NAME: me - 1}, device_id_type=pl.DeviceIdType.MESH).start()

    def sent_rows(kind):
        @pl.when(me + 1 < n)
        def _():
            relay(kind, 0, True).wait_send()

        @pl.when(me > 0)
        def _():
            pltpu.make_async_remote_copy(
                src_ref=rows_all.at[kind, me], dst_ref=rows_all.at[kind, me],
                send_sem=left_s.at[kind], recv_sem=rows_r.at[kind, me],
                device_id={T_NAME: me - 1}, device_id_type=pl.DeviceIdType.MESH).wait_send()

        for hop in range(1, n):
            for right in (True, False):
                @pl.when(goes(hop, right))
                def _():
                    relay(kind, hop, right).wait_send()

    def walk(kind, use):
        use(me, True)
        for hop in range(1, n):
            for right in (True, False):
                @pl.when(comes(hop, right))
                def _():
                    block = me - hop if right else me + hop
                    arrive(rows_all.at[kind, block], rows_r.at[kind, block])

                @pl.when(goes(hop, right))
                def _():
                    relay(kind, hop, right).start()

            for right in (True, False):
                @pl.when(comes(hop, right))
                def _():
                    use(me - hop if right else me + hop, False)

    def to_peers(src, dst, s, r):
        for step in range(1, n):
            send(src, dst, s.at[step], r.at[me], {T_NAME: lax.rem(me + step, n)})

    def from_peers(buf, r):
        for step in range(1, n):
            block = lax.rem(me + n - step, n)
            arrive(buf.at[block], r.at[block])

    rows_all[0, me] = lat_ref[...]
    stat_mine[0] = pack_moments(lat_ref[...].astype(f32))
    for level in range(2):
        rows = sum(jnp.where(step_ref[0] == s, table_ref[level, s].astype(f32), 0.0) for s in range(table_ref.shape[1]))
        gates[level : level + 1, :] = rows[2:3]
        for row in range(2):
            for j in range(lane_rows):
                place = (2 * level + row) * lane_rows + j
                mod_mine[place : place + 1, :] = rows[row : row + 1, j * LANES : (j + 1) * LANES]
    barrier = pltpu.get_barrier_semaphore()
    for step in range(1, n):
        pl.semaphore_signal(barrier, inc=1, device_id={T_NAME: lax.rem(me + step, n)}, device_id_type=pl.DeviceIdType.MESH)
    for step in range(1, nb):
        pl.semaphore_signal(barrier, inc=1, device_id={B_NAME: lax.rem(mb + step, nb)}, device_id_type=pl.DeviceIdType.MESH)
    pl.semaphore_wait(barrier, n - 1 + nb - 1)

    to_peers(stat_mine.at[0], stat_all.at[0, me], stat_s.at[0], stat_r.at[0])
    to_peers(mod_mine, mod_all.at[me], mod_s, mod_r)
    own_rows(0)
    spot = pl.ds(pl.multiple_of(mb * part, 16), part)
    for level in range(2):
        for step in range(1, nb):
            send(ad_ref.at[level], ad_all.at[level, spot, :], ad_s.at[level, step], ad_r.at[level, mb], {B_NAME: lax.rem(mb + step, nb)})
    mod_all[me] = mod_mine[...]
    ad_all[:, spot, :] = ad_ref[...]
    stat_all[0, me] = stat_mine[0]

    def wait_ad(level):
        for step in range(1, nb):
            other = lax.rem(mb + step, nb)
            there = pl.ds(pl.multiple_of(other * part, 16), part)
            arrive(ad_all.at[level, there, :], ad_r.at[level, other])

    def statistics(kind):
        parts = [unpack_moments(stat_all[kind, b], count) for b in range(n)]
        mean = sum(p[0] for p in parts) * (1.0 / n)
        square = sum(p[1] + width * (p[0] - mean) * (p[0] - mean) for p in parts)
        return mean, lax.rsqrt(square * (1.0 / (n * width)) + 1e-06)

    def mod_row(block, row):
        return jnp.concatenate([mod_all[block, row * lane_rows + j : row * lane_rows + j + 1, :] for j in range(lane_rows)], axis=1)

    def apply(kind, level, block, stats):
        values = rows_all[kind, block].astype(f32)
        return ((values - stats[0]) * stats[1] * (1.0 + mod_row(block, 2 * level + 1)) + mod_row(block, 2 * level)).astype(bf16)

    def up_step(slot, target, init):
        def body(start, size):
            columns = pl.ds(start, size)
            value = jnp.dot(normed[...], up_buf[slot, :, columns], preferred_element_type=f32)
            if init:
                hid[target, :, columns] = value
            else:
                hid[target, :, columns] += value

        matmul_tiles(units, 512, body)

    def add_low(target, low):
        def body(start, size):
            columns = pl.ds(start, size)
            hid[target, :, columns] += jnp.dot(low, uo_ref[:, columns], preferred_element_type=f32)

        matmul_tiles(units, 512, body)

    half = lax.broadcasted_iota(jnp.int32, (count, LANES), 1) < LANES // 2

    def low_sum(kind):
        return sum(low_all[kind, b].astype(f32) for b in range(n))

    def back_projection(level):
        value = jnp.dot(act[...], di_ref[level], preferred_element_type=f32)
        mine = half if level == 1 else jnp.logical_not(half)
        back_mine[level] = jnp.where(mine, jnp.concatenate([value, value], axis=1), 0.0).astype(bf16)
        back_all[level, me] = back_mine[level]
        to_peers(back_mine.at[level], back_all.at[level, me], back_s.at[level], back_r.at[level])

    def down_steps(level):
        for step in range(n):
            down_copy(level, step).wait()

            def body(start, size):
                columns = pl.ds(start, size)
                value = jnp.dot(act[...], down_buf[step, :, columns], preferred_element_type=f32)
                if step < n - 1:
                    sums_out[level, step, :, columns] = value.astype(bf16)
                else:
                    own[:, columns] = value

            matmul_tiles(width, 256, body)
            if step < n - 1:
                send(sums_out.at[level, step], sums_in.at[level, me], sum_s.at[level, step], sum_r.at[level, me], {T_NAME: lax.rem(me + 1 + step, n)})
            if step == 0:
                back_projection(level)
            if level == 0:
                down_copy(1, step).start()

    def settle(level):
        from_peers(back_all.at[level], back_r.at[level])
        low = sum(back_all[level, b].astype(f32) for b in range(n)).astype(bf16)
        total = own[...] + lax.dot_general(low, ad_all[level], (((1,), (1,)), ((), ())), preferred_element_type=f32)
        from_peers(sums_in.at[level], sum_r.at[level])
        for step in range(1, n):
            total = total + sums_in[level, lax.rem(me + step, n)].astype(f32)
        return total

    from_peers(stat_all.at[0], stat_r.at[0])
    from_peers(mod_all, mod_r)
    lat_stats = statistics(0)
    wait_ad(0)
    low0 = jnp.dot(apply(0, 0, me, lat_stats), ad_all[0], preferred_element_type=f32)
    wait_ad(1)
    low1 = jnp.dot(apply(0, 1, me, lat_stats), ad_all[1], preferred_element_type=f32)
    low_mine[0] = jnp.where(half, low0, low1).astype(bf16)
    low_all[0, me] = low_mine[0]
    to_peers(low_mine.at[0], low_all.at[0, me], low_s.at[0], low_r.at[0])

    def use_latent(block, init):
        normed[...] = apply(0, 0, block, lat_stats)
        up_copy(0, block).wait()
        up_step(up_slot(0, block), 0, init)

    walk(0, use_latent)
    for block in range(up_slots - n, n):
        up_copy(1, block).start()
    from_peers(low_all.at[0], low_r.at[0])
    add_low(0, jnp.where(half, low_sum(0), 0.0).astype(bf16))
    act[...] = jax.nn.gelu(hid[0], approximate=True).astype(bf16)
    down_steps(0)
    for block in range(n):
        normed[...] = apply(0, 1, block, lat_stats)
        up_copy(1, block).wait()
        up_step((n + block) % up_slots, 1, block == 0)
    add_low(1, jnp.where(half, 0.0, low_sum(0)).astype(bf16))
    hid[1] = jax.nn.gelu(hid[1], approximate=True)
    first = (lat_ref[...].astype(f32) + gates[0:1, :] * settle(0)).astype(bf16)
    rows_all[1, me] = first
    stat_mine[1] = pack_moments(first.astype(f32))
    to_peers(stat_mine.at[1], stat_all.at[1, me], stat_s.at[1], stat_r.at[1])
    own_rows(1)
    stat_all[1, me] = stat_mine[1]
    from_peers(stat_all.at[1], stat_r.at[1])
    stats = statistics(1)
    low = jnp.dot(apply(1, 1, me, stats), ad_all[1], preferred_element_type=f32)
    low_mine[1] = jnp.where(half, 0.0, low).astype(bf16)
    low_all[1, me] = low_mine[1]
    to_peers(low_mine.at[1], low_all.at[1, me], low_s.at[1], low_r.at[1])

    def use_first(block, init):
        normed[...] = apply(1, 1, block, stats)
        up_step(up_slot(1, block), 0, init)

    walk(1, use_first)
    from_peers(low_all.at[1], low_r.at[1])
    add_low(0, low_sum(1).astype(bf16))
    active = jax.nn.gelu(hid[0], approximate=True)
    act[...] = ((1.0 + guide_weight) * active - (guide_weight * keep) * hid[1]).astype(bf16)
    down_steps(1)
    total = settle(1)
    first_value = rows_all[1, me].astype(f32)
    start = first_value + guide_weight * keep * (first_value - lat_ref[...].astype(f32))
    out_ref[...] = (start + gates[1:2, :] * total).astype(out_ref.dtype)
    for kind in range(2):
        sent_rows(kind)
    for copy in sent:
        copy.wait_send()


def per_device_fused(n, nb, latent, mod_table, skip_layer, step_index, up_weight, down_weight, up_in, up_out, down_in, down_out):
    f32, bf16 = jnp.float32, jnp.bfloat16
    tokens = latent[0]
    count, width = tokens.shape
    units = up_weight.shape[2]
    keep = (skip_layer == 0).astype(f32)
    lane_rows = 4 * width // LANES
    turned = jnp.swapaxes(down_out, 1, 2)
    ad = jnp.stack([jnp.concatenate([up_in[0], turned[0]], axis=1), jnp.concatenate([turned[1], up_in[1]], axis=1)])
    uo = up_out.reshape(LANES, units)
    up_slots = n + 2
    vmem = pl.BlockSpec(memory_space=pltpu.VMEM)
    hbm = pl.BlockSpec(memory_space=pl.ANY)
    dma = pltpu.SemaphoreType.DMA
    part = ad.shape[1]
    return pl.pallas_call(
        functools.partial(window_kernel, n, nb),
        out_shape=jax.ShapeDtypeStruct((count, width), bf16),
        in_specs=[pl.BlockSpec(memory_space=pltpu.SMEM)] * 2 + [vmem] * 5 + [hbm] * 2,
        out_specs=vmem,
        scratch_shapes=[
            pltpu.VMEM((2, n, count, width), bf16),
            pltpu.VMEM((lane_rows, LANES), f32),
            pltpu.VMEM((8, width), f32),
            pltpu.VMEM((n, lane_rows, LANES), f32),
            pltpu.VMEM((2, n, 8, LANES), f32),
            pltpu.VMEM((2, n, count, LANES), bf16),
            pltpu.VMEM((2, n, count, LANES), bf16),
            pltpu.VMEM((2, part * nb, LANES), bf16),
            pltpu.VMEM((2, n, count, width), bf16),
            pltpu.VMEM((2, n - 1, count, width), bf16),
            pltpu.VMEM((count, width), bf16),
            pltpu.VMEM((count, units), bf16),
            pltpu.VMEM((2, count, units), f32),
            pltpu.VMEM((count, width), f32),
            pltpu.VMEM((2, 8, LANES), f32),
            pltpu.VMEM((2, count, LANES), bf16),
            pltpu.VMEM((2, count, LANES), bf16),
            pltpu.VMEM((up_slots, width, units), bf16),
            pltpu.VMEM((n, units, width), bf16),
            dma((2 * n,)), dma((2 * n,)),
            dma((2, n)), dma((2, n)),
            dma((n,)), dma((n,)),
            dma((2, n)), dma((2, n)),
            dma((2, n)), dma((2, n)),
            dma((2, n)), dma((2, n)),
            dma((2, nb)), dma((2, nb)),
            dma((2, n)), dma((2, n)),
            dma((2,)),
        ],
        compiler_params=pltpu.CompilerParams(collective_id=0, has_side_effects=True, vmem_limit_bytes=63 * 2**20),
        cost_estimate=pl.CostEstimate(flops=8 * 10**9, bytes_accessed=80 * 10**6, transcendentals=400000),
    )(keep, step_index, tokens, mod_table, ad, uo, down_in, up_weight, down_weight)[None]


def solution(mesh):
    placed = (
        P(("groups", "batch"), None, "tensor"),
        P(None, None, None, "tensor"),
        P(("groups", "batch")),
        P(("groups", "batch")),
        P(None, None, "tensor"),
        P(None, "tensor", None),
        P(None, ("tensor", "batch"), None),
        P(None, None, "tensor"),
        P(None, "tensor", None),
        P(None, None, ("tensor", "batch")),
    )
    n, nb = mesh.shape["tensor"], mesh.shape["batch"]

    def one_device(*arrays):
        latent, up_weight, up_out = arrays[0], arrays[4], arrays[7]
        count, width = latent.shape[1:]
        units, rank = up_weight.shape[2], up_out.shape[1]
        aligned = width % LANES == 0 and units % LANES == 0 and 2 * rank == LANES
        small = n * width * units * 2 <= 20 * 2**20 and n > 2 and nb > 1
        if aligned and small and count % 16 == 0 and count <= LANES:
            return per_device_fused(n, nb, *arrays)
        return per_device(*arrays)

    return jax.shard_map(
        one_device,
        mesh=mesh,
        in_specs=placed,
        out_specs=P(("groups", "batch"), None, "tensor"),
        check_vma=False,
    )
```

```python
import functools

import jax
import jax.numpy as jnp
from jax import lax
from jax.experimental import pallas as pl
from jax.experimental.pallas import tpu as pltpu
from jax.sharding import PartitionSpec as P

guide_weight = 1.0


def modulate(rows, mod):
    values = rows.astype(jnp.float32)
    center = values - jnp.mean(values, axis=-1, keepdims=True)
    spread = jnp.mean(center * center, axis=-1, keepdims=True)
    normed = center * lax.rsqrt(spread + 1e-06)
    return (normed * (1.0 + mod[1]) + mod[0]).astype(jnp.bfloat16)


def dot32(a, b):
    return jnp.dot(a, b, preferred_element_type=jnp.float32)


def own_columns(array, width):
    start = lax.axis_index("tensor") * width
    return lax.dynamic_slice_in_dim(array, start, width, axis=1)


def hidden_of(rows, mod, w_up, a_own, up_out):
    normed = modulate(rows, mod)
    low = lax.psum(dot32(own_columns(normed, a_own.shape[0]), a_own), "tensor")
    return dot32(normed, w_up) + dot32(low.astype(jnp.bfloat16), up_out)


def project_down(active, w_down, down_in, d_own):
    low = lax.psum(dot32(active, down_in), "tensor")
    total = lax.psum_scatter(dot32(active, w_down), "tensor", scatter_dimension=1, tiled=True)
    return total + dot32(low.astype(jnp.bfloat16), d_own)


def gelu(x):
    return jax.nn.gelu(x, approximate=True)


def per_device(
    latent,
    mod_table,
    skip_layer,
    step_index,
    up_weight,
    down_weight,
    up_in,
    up_out,
    down_in,
    down_out,
):
    tokens = latent[0]
    keep = (skip_layer[0] == 0).astype(jnp.float32)
    mods = lax.dynamic_index_in_dim(mod_table, step_index[0], axis=1, keepdims=False)
    mods_local = mods.astype(jnp.float32)
    a_own = lax.all_gather(up_in, "batch", axis=1, tiled=True)
    d_own = lax.all_gather(down_out, "batch", axis=2, tiled=True)
    tokens_full = lax.all_gather(tokens, "tensor", axis=1, tiled=True)
    mods_full = lax.all_gather(mods[:, :2], "tensor", axis=2, tiled=True).astype(jnp.float32)
    hidden = hidden_of(tokens_full, mods_full[0], up_weight[0], a_own[0], up_out[0])
    active = gelu(hidden).astype(jnp.bfloat16)
    first_sum = project_down(active, down_weight[0], down_in[0], d_own[0])
    token_value = tokens.astype(jnp.float32)
    first = (token_value + mods_local[0, 2] * first_sum).astype(jnp.bfloat16)
    first_full = lax.all_gather(first, "tensor", axis=1, tiled=True)
    count = tokens.shape[0]
    stacked = jnp.concatenate([first_full, tokens_full], axis=0)
    hidden = gelu(hidden_of(stacked, mods_full[1], up_weight[1], a_own[1], up_out[1]))
    active = ((1.0 + guide_weight) * hidden[:count] - (guide_weight * keep) * hidden[count:]).astype(jnp.bfloat16)
    summed = project_down(active, down_weight[1], down_in[1], d_own[1])
    first_value = first.astype(jnp.float32)
    start = first_value + guide_weight * keep * (first_value - token_value)
    return (start + mods_local[1, 2] * summed).astype(jnp.bfloat16)[None]


T_NAME = "tensor"
B_NAME = "batch"
LANES = 128


def matmul_tiles(width, tile, body):
    whole = width // tile

    @pl.loop(0, whole)
    def _(i):
        body(pl.multiple_of(i * tile, tile), tile)

    if width % tile:
        body(whole * tile, width % tile)


def moments(values):
    mean = jnp.mean(values, axis=-1, keepdims=True)
    center = values - mean
    return mean, jnp.sum(center * center, axis=-1, keepdims=True)


def pack_moments(values):
    mean, square = moments(values)
    count = values.shape[0]
    lane = lax.broadcasted_iota(jnp.int32, (count, LANES), 1)
    both = jnp.where(lane == 0, mean, jnp.where(lane == 1, square, 0.0))
    if count < LANES:
        both = jnp.concatenate([both, jnp.zeros((LANES - count, LANES), jnp.float32)], axis=0)
    return both.T[:8]


def unpack_moments(packed, count):
    whole = jnp.concatenate([packed, jnp.zeros((LANES - 8, LANES), jnp.float32)], axis=0).T
    return whole[:count, 0:1], whole[:count, 1:2]


def window_kernel(
    n, nb,
    keep_ref, step_ref, lat_ref, table_ref, ui_ref, do_ref, uo_ref, di_ref, uw, dw,
    out_ref,
    ad_ref, rows_all, mod_mine, gates, mod_all, stat_all, low_all, back_all, ad_all, sums_in, sums_out,
    normed, act, hid, own, stat_mine, low_mine, back_mine,
    up_buf, down_buf,
    up_sem, down_sem,
    rows_s, rows_r, mod_s, mod_r, stat_s, stat_r, low_s, low_r, back_s, back_r, ad_s, ad_r, sum_s, sum_r, left_s,
):
    me = lax.axis_index(T_NAME)
    mb = lax.axis_index(B_NAME)
    count, width = lat_ref.shape
    units = uo_ref.shape[1]
    part = ad_ref.shape[1]
    up_slots = up_buf.shape[0]
    lane_rows = width // LANES
    keep = keep_ref[0]
    f32, bf16 = jnp.float32, jnp.bfloat16

    def up_slot(level, block):
        return lax.rem(level * n + block, up_slots)

    def up_copy(level, block):
        rows = pl.ds(pl.multiple_of(block * width, LANES), width)
        return pltpu.make_async_copy(uw.at[level, rows, :], up_buf.at[up_slot(level, block)], up_sem.at[level * n + block])

    def down_copy(level, step):
        block = lax.rem(me + 1 + step, n)
        columns = pl.ds(pl.multiple_of(block * width, LANES), width)
        return pltpu.make_async_copy(dw.at[level, :, columns], down_buf.at[step], down_sem.at[level * n + step])

    for step in range(n):
        up_copy(0, lax.rem(me + step, n)).start()
    for step in range(n):
        down_copy(0, step).start()
    for step in range(up_slots - n):
        up_copy(1, step).start()

    sent = []

    def send(src, dst, s, r, where):
        copy = pltpu.make_async_remote_copy(
            src_ref=src, dst_ref=dst, send_sem=s, recv_sem=r,
            device_id=where, device_id_type=pl.DeviceIdType.MESH)
        copy.start()
        sent.append(copy)

    def arrive(buf, r):
        pltpu.make_async_remote_copy(
            src_ref=buf, dst_ref=buf, send_sem=r, recv_sem=r,
            device_id={T_NAME: lax.rem(me + 1, n)}, device_id_type=pl.DeviceIdType.MESH).wait_recv()

    def relay(kind, hop, right):
        block, target = (me - hop, me + 1) if right else (me + hop, me - 1)
        return pltpu.make_async_remote_copy(
            src_ref=rows_all.at[kind, block], dst_ref=rows_all.at[kind, block],
            send_sem=rows_s.at[kind, block], recv_sem=rows_r.at[kind, block],
            device_id={T_NAME: target}, device_id_type=pl.DeviceIdType.MESH)

    def comes(hop, right):
        return me >= hop if right else me + hop < n

    def goes(hop, right):
        return jnp.logical_and(me >= hop, me + 1 < n) if right else jnp.logical_and(me + hop < n, me > 0)

    def own_rows(kind):
        @pl.when(me + 1 < n)
        def _():
            relay(kind, 0, True).start()

        @pl.when(me > 0)
        def _():
            pltpu.make_async_remote_copy(
                src_ref=rows_all.at[kind, me], dst_ref=rows_all.at[kind, me],
                send_sem=left_s.at[kind], recv_sem=rows_r.at[kind, me],
                device_id={T_NAME: me - 1}, device_id_type=pl.DeviceIdType.MESH).start()

    def sent_rows(kind):
        @pl.when(me + 1 < n)
        def _():
            relay(kind, 0, True).wait_send()

        @pl.when(me > 0)
        def _():
            pltpu.make_async_remote_copy(
                src_ref=rows_all.at[kind, me], dst_ref=rows_all.at[kind, me],
                send_sem=left_s.at[kind], recv_sem=rows_r.at[kind, me],
                device_id={T_NAME: me - 1}, device_id_type=pl.DeviceIdType.MESH).wait_send()

        for hop in range(1, n):
            for right in (True, False):
                @pl.when(goes(hop, right))
                def _():
                    relay(kind, hop, right).wait_send()

    def walk(kind, use):
        use(me, True)
        for hop in range(1, n):
            for right in (True, False):
                @pl.when(comes(hop, right))
                def _():
                    block = me - hop if right else me + hop
                    arrive(rows_all.at[kind, block], rows_r.at[kind, block])

                @pl.when(goes(hop, right))
                def _():
                    relay(kind, hop, right).start()

            for right in (True, False):
                @pl.when(comes(hop, right))
                def _():
                    use(me - hop if right else me + hop, False)

    def to_peers(src, dst, s, r):
        for step in range(1, n):
            send(src, dst, s.at[step], r.at[me], {T_NAME: lax.rem(me + step, n)})

    def from_peers(buf, r):
        for step in range(1, n):
            block = lax.rem(me + n - step, n)
            arrive(buf.at[block], r.at[block])

    rows_all[0, me] = lat_ref[...]
    stat_mine[0] = pack_moments(lat_ref[...].astype(f32))
    for level in range(2):
        chosen = lax.broadcasted_iota(jnp.int32, table_ref.shape[2:], 0) == step_ref[0]
        picked = [jnp.sum(jnp.where(chosen, table_ref[level, row].astype(f32), 0.0), axis=0, keepdims=True) for row in range(3)]
        gates[level : level + 1, :] = picked[2]
        both = [ui_ref[level].astype(f32), do_ref[level].astype(f32)]
        ad_ref[level] = jnp.concatenate(both if level == 0 else both[::-1], axis=0).T.astype(bf16)
        for row in range(2):
            for j in range(lane_rows):
                place = (2 * level + row) * lane_rows + j
                mod_mine[place : place + 1, :] = picked[row][:, j * LANES : (j + 1) * LANES]
    barrier = pltpu.get_barrier_semaphore()
    for step in range(1, n):
        pl.semaphore_signal(barrier, inc=1, device_id={T_NAME: lax.rem(me + step, n)}, device_id_type=pl.DeviceIdType.MESH)
    for step in range(1, nb):
        pl.semaphore_signal(barrier, inc=1, device_id={B_NAME: lax.rem(mb + step, nb)}, device_id_type=pl.DeviceIdType.MESH)
    pl.semaphore_wait(barrier, n - 1 + nb - 1)

    to_peers(stat_mine.at[0], stat_all.at[0, me], stat_s.at[0], stat_r.at[0])
    to_peers(mod_mine, mod_all.at[me], mod_s, mod_r)
    own_rows(0)
    spot = pl.ds(pl.multiple_of(mb * part, 16), part)
    for level in range(2):
        for step in range(1, nb):
            send(ad_ref.at[level], ad_all.at[level, spot, :], ad_s.at[level, step], ad_r.at[level, mb], {B_NAME: lax.rem(mb + step, nb)})
    mod_all[me] = mod_mine[...]
    ad_all[:, spot, :] = ad_ref[...]
    stat_all[0, me] = stat_mine[0]

    def wait_ad(level):
        for step in range(1, nb):
            other = lax.rem(mb + step, nb)
            there = pl.ds(pl.multiple_of(other * part, 16), part)
            arrive(ad_all.at[level, there, :], ad_r.at[level, other])

    def statistics(kind):
        parts = [unpack_moments(stat_all[kind, b], count) for b in range(n)]
        mean = sum(p[0] for p in parts) * (1.0 / n)
        square = sum(p[1] + width * (p[0] - mean) * (p[0] - mean) for p in parts)
        return mean, lax.rsqrt(square * (1.0 / (n * width)) + 1e-06)

    def mod_row(block, row):
        return jnp.concatenate([mod_all[block, row * lane_rows + j : row * lane_rows + j + 1, :] for j in range(lane_rows)], axis=1)

    def apply(kind, level, block, stats):
        values = rows_all[kind, block].astype(f32)
        return ((values - stats[0]) * stats[1] * (1.0 + mod_row(block, 2 * level + 1)) + mod_row(block, 2 * level)).astype(bf16)

    def up_step(slot, target, init):
        def body(start, size):
            columns = pl.ds(start, size)
            value = jnp.dot(normed[...], up_buf[slot, :, columns], preferred_element_type=f32)
            if init:
                hid[target, :, columns] = value
            else:
                hid[target, :, columns] += value

        matmul_tiles(units, 512, body)

    def add_low(target, low):
        def body(start, size):
            columns = pl.ds(start, size)
            hid[target, :, columns] += jnp.dot(low, uo_ref[:, columns], preferred_element_type=f32)

        matmul_tiles(units, 512, body)

    half = lax.broadcasted_iota(jnp.int32, (count, LANES), 1) < LANES // 2

    def low_sum(kind):
        return sum(low_all[kind, b].astype(f32) for b in range(n))

    def back_projection(level):
        value = lax.dot_general(act[...], di_ref[level], (((1,), (1,)), ((), ())), preferred_element_type=f32)
        mine = half if level == 1 else jnp.logical_not(half)
        back_mine[level] = jnp.where(mine, jnp.concatenate([value, value], axis=1), 0.0).astype(bf16)
        back_all[level, me] = back_mine[level]
        to_peers(back_mine.at[level], back_all.at[level, me], back_s.at[level], back_r.at[level])

    def down_steps(level):
        for step in range(n):
            down_copy(level, step).wait()

            def body(start, size):
                columns = pl.ds(start, size)
                value = jnp.dot(act[...], down_buf[step, :, columns], preferred_element_type=f32)
                if step < n - 1:
                    sums_out[level, step, :, columns] = value.astype(bf16)
                else:
                    own[:, columns] = value

            matmul_tiles(width, 256, body)
            if step < n - 1:
                send(sums_out.at[level, step], sums_in.at[level, me], sum_s.at[level, step], sum_r.at[level, me], {T_NAME: lax.rem(me + 1 + step, n)})
            if step == 0:
                back_projection(level)
            if level == 0:
                down_copy(1, step).start()

    def settle(level):
        from_peers(back_all.at[level], back_r.at[level])
        low = sum(back_all[level, b].astype(f32) for b in range(n)).astype(bf16)
        total = own[...] + lax.dot_general(low, ad_all[level], (((1,), (1,)), ((), ())), preferred_element_type=f32)
        from_peers(sums_in.at[level], sum_r.at[level])
        for step in range(1, n):
            total = total + sums_in[level, lax.rem(me + step, n)].astype(f32)
        return total

    from_peers(stat_all.at[0], stat_r.at[0])
    from_peers(mod_all, mod_r)
    lat_stats = statistics(0)
    wait_ad(0)
    low0 = jnp.dot(apply(0, 0, me, lat_stats), ad_all[0], preferred_element_type=f32)
    wait_ad(1)
    low1 = jnp.dot(apply(0, 1, me, lat_stats), ad_all[1], preferred_element_type=f32)
    low_mine[0] = jnp.where(half, low0, low1).astype(bf16)
    low_all[0, me] = low_mine[0]
    to_peers(low_mine.at[0], low_all.at[0, me], low_s.at[0], low_r.at[0])

    def use_latent(block, init):
        normed[...] = apply(0, 0, block, lat_stats)
        up_copy(0, block).wait()
        up_step(up_slot(0, block), 0, init)

    walk(0, use_latent)
    for block in range(up_slots - n, n):
        up_copy(1, block).start()
    from_peers(low_all.at[0], low_r.at[0])
    add_low(0, jnp.where(half, low_sum(0), 0.0).astype(bf16))
    act[...] = jax.nn.gelu(hid[0], approximate=True).astype(bf16)
    down_steps(0)
    for block in range(n):
        normed[...] = apply(0, 1, block, lat_stats)
        up_copy(1, block).wait()
        up_step((n + block) % up_slots, 1, block == 0)
    add_low(1, jnp.where(half, 0.0, low_sum(0)).astype(bf16))
    hid[1] = jax.nn.gelu(hid[1], approximate=True)
    first = (lat_ref[...].astype(f32) + gates[0:1, :] * settle(0)).astype(bf16)
    rows_all[1, me] = first
    stat_mine[1] = pack_moments(first.astype(f32))
    to_peers(stat_mine.at[1], stat_all.at[1, me], stat_s.at[1], stat_r.at[1])
    own_rows(1)
    stat_all[1, me] = stat_mine[1]
    from_peers(stat_all.at[1], stat_r.at[1])
    stats = statistics(1)
    low = jnp.dot(apply(1, 1, me, stats), ad_all[1], preferred_element_type=f32)
    low_mine[1] = jnp.where(half, 0.0, low).astype(bf16)
    low_all[1, me] = low_mine[1]
    to_peers(low_mine.at[1], low_all.at[1, me], low_s.at[1], low_r.at[1])

    def use_first(block, init):
        normed[...] = apply(1, 1, block, stats)
        up_step(up_slot(1, block), 0, init)

    walk(1, use_first)
    from_peers(low_all.at[1], low_r.at[1])
    add_low(0, low_sum(1).astype(bf16))
    active = jax.nn.gelu(hid[0], approximate=True)
    act[...] = ((1.0 + guide_weight) * active - (guide_weight * keep) * hid[1]).astype(bf16)
    down_steps(1)
    total = settle(1)
    first_value = rows_all[1, me].astype(f32)
    start = first_value + guide_weight * keep * (first_value - lat_ref[...].astype(f32))
    out_ref[...] = (start + gates[1:2, :] * total).astype(out_ref.dtype)
    for kind in range(2):
        sent_rows(kind)
    for copy in sent:
        copy.wait_send()


def per_device_fused(n, nb, latent, mod_table, skip_layer, step_index, up_weight, down_weight, up_in, up_out, down_in, down_out):
    f32, bf16 = jnp.float32, jnp.bfloat16
    tokens = latent[0]
    count, width = tokens.shape
    units = up_weight.shape[2]
    keep = (skip_layer == 0).astype(f32)
    lane_rows = 4 * width // LANES
    uo = up_out.reshape(LANES, units)
    up_slots = n + 2
    vmem = pl.BlockSpec(memory_space=pltpu.VMEM)
    hbm = pl.BlockSpec(memory_space=pl.ANY)
    dma = pltpu.SemaphoreType.DMA
    part = up_in.shape[1]
    return pl.pallas_call(
        functools.partial(window_kernel, n, nb),
        out_shape=jax.ShapeDtypeStruct((count, width), bf16),
        in_specs=[pl.BlockSpec(memory_space=pltpu.SMEM)] * 2 + [vmem] * 6 + [hbm] * 2,
        out_specs=vmem,
        scratch_shapes=[
            pltpu.VMEM((2, part, LANES), bf16),
            pltpu.VMEM((2, n, count, width), bf16),
            pltpu.VMEM((lane_rows, LANES), f32),
            pltpu.VMEM((8, width), f32),
            pltpu.VMEM((n, lane_rows, LANES), f32),
            pltpu.VMEM((2, n, 8, LANES), f32),
            pltpu.VMEM((2, n, count, LANES), bf16),
            pltpu.VMEM((2, n, count, LANES), bf16),
            pltpu.VMEM((2, part * nb, LANES), bf16),
            pltpu.VMEM((2, n, count, width), bf16),
            pltpu.VMEM((2, n - 1, count, width), bf16),
            pltpu.VMEM((count, width), bf16),
            pltpu.VMEM((count, units), bf16),
            pltpu.VMEM((2, count, units), f32),
            pltpu.VMEM((count, width), f32),
            pltpu.VMEM((2, 8, LANES), f32),
            pltpu.VMEM((2, count, LANES), bf16),
            pltpu.VMEM((2, count, LANES), bf16),
            pltpu.VMEM((up_slots, width, units), bf16),
            pltpu.VMEM((n, units, width), bf16),
            dma((2 * n,)), dma((2 * n,)),
            dma((2, n)), dma((2, n)),
            dma((n,)), dma((n,)),
            dma((2, n)), dma((2, n)),
            dma((2, n)), dma((2, n)),
            dma((2, n)), dma((2, n)),
            dma((2, nb)), dma((2, nb)),
            dma((2, n)), dma((2, n)),
            dma((2,)),
        ],
        compiler_params=pltpu.CompilerParams(collective_id=0, has_side_effects=True, vmem_limit_bytes=63 * 2**20),
        cost_estimate=pl.CostEstimate(flops=8 * 10**9, bytes_accessed=80 * 10**6, transcendentals=400000),
    )(keep, step_index, tokens, jnp.swapaxes(mod_table, 1, 2), jnp.swapaxes(up_in, 1, 2), down_out, uo, jnp.swapaxes(down_in, 1, 2), up_weight, down_weight)[None]


def solution(mesh):
    placed = (
        P(("groups", "batch"), None, "tensor"),
        P(None, None, None, "tensor"),
        P(("groups", "batch")),
        P(("groups", "batch")),
        P(None, None, "tensor"),
        P(None, "tensor", None),
        P(None, ("tensor", "batch"), None),
        P(None, None, "tensor"),
        P(None, "tensor", None),
        P(None, None, ("tensor", "batch")),
    )
    n, nb = mesh.shape["tensor"], mesh.shape["batch"]

    def one_device(*arrays):
        latent, up_weight, up_out = arrays[0], arrays[4], arrays[7]
        count, width = latent.shape[1:]
        units, rank = up_weight.shape[2], up_out.shape[1]
        aligned = width % LANES == 0 and units % LANES == 0 and 2 * rank == LANES
        small = n * width * units * 2 <= 20 * 2**20 and n > 2 and nb > 1
        if aligned and small and count % 16 == 0 and count <= LANES:
            return per_device_fused(n, nb, *arrays)
        return per_device(*arrays)

    return jax.shard_map(
        one_device,
        mesh=mesh,
        in_specs=placed,
        out_specs=P(("groups", "batch"), None, "tensor"),
        check_vma=False,
    )
```

```python
import functools

import jax
import jax.numpy as jnp
from jax import lax
from jax.experimental import pallas as pl
from jax.experimental.pallas import tpu as pltpu
from jax.sharding import PartitionSpec as P

guide_weight = 1.0


def modulate(rows, mod):
    values = rows.astype(jnp.float32)
    center = values - jnp.mean(values, axis=-1, keepdims=True)
    spread = jnp.mean(center * center, axis=-1, keepdims=True)
    normed = center * lax.rsqrt(spread + 1e-06)
    return (normed * (1.0 + mod[1]) + mod[0]).astype(jnp.bfloat16)


def dot32(a, b):
    return jnp.dot(a, b, preferred_element_type=jnp.float32)


def own_columns(array, width):
    start = lax.axis_index("tensor") * width
    return lax.dynamic_slice_in_dim(array, start, width, axis=1)


def hidden_of(rows, mod, w_up, a_own, up_out):
    normed = modulate(rows, mod)
    low = lax.psum(dot32(own_columns(normed, a_own.shape[0]), a_own), "tensor")
    return dot32(normed, w_up) + dot32(low.astype(jnp.bfloat16), up_out)


def project_down(active, w_down, down_in, d_own):
    low = lax.psum(dot32(active, down_in), "tensor")
    total = lax.psum_scatter(dot32(active, w_down), "tensor", scatter_dimension=1, tiled=True)
    return total + dot32(low.astype(jnp.bfloat16), d_own)


def gelu(x):
    return jax.nn.gelu(x, approximate=True)


def per_device(
    latent,
    mod_table,
    skip_layer,
    step_index,
    up_weight,
    down_weight,
    up_in,
    up_out,
    down_in,
    down_out,
):
    tokens = latent[0]
    keep = (skip_layer[0] == 0).astype(jnp.float32)
    mods = lax.dynamic_index_in_dim(mod_table, step_index[0], axis=1, keepdims=False)
    mods_local = mods.astype(jnp.float32)
    a_own = lax.all_gather(up_in, "batch", axis=1, tiled=True)
    d_own = lax.all_gather(down_out, "batch", axis=2, tiled=True)
    tokens_full = lax.all_gather(tokens, "tensor", axis=1, tiled=True)
    mods_full = lax.all_gather(mods[:, :2], "tensor", axis=2, tiled=True).astype(jnp.float32)
    hidden = hidden_of(tokens_full, mods_full[0], up_weight[0], a_own[0], up_out[0])
    active = gelu(hidden).astype(jnp.bfloat16)
    first_sum = project_down(active, down_weight[0], down_in[0], d_own[0])
    token_value = tokens.astype(jnp.float32)
    first = (token_value + mods_local[0, 2] * first_sum).astype(jnp.bfloat16)
    first_full = lax.all_gather(first, "tensor", axis=1, tiled=True)
    count = tokens.shape[0]
    stacked = jnp.concatenate([first_full, tokens_full], axis=0)
    hidden = gelu(hidden_of(stacked, mods_full[1], up_weight[1], a_own[1], up_out[1]))
    active = ((1.0 + guide_weight) * hidden[:count] - (guide_weight * keep) * hidden[count:]).astype(jnp.bfloat16)
    summed = project_down(active, down_weight[1], down_in[1], d_own[1])
    first_value = first.astype(jnp.float32)
    start = first_value + guide_weight * keep * (first_value - token_value)
    return (start + mods_local[1, 2] * summed).astype(jnp.bfloat16)[None]


T_NAME = "tensor"
B_NAME = "batch"
LANES = 128


def matmul_tiles(width, tile, body):
    whole = width // tile

    @pl.loop(0, whole)
    def _(i):
        body(pl.multiple_of(i * tile, tile), tile)

    if width % tile:
        body(whole * tile, width % tile)


def moments(values):
    mean = jnp.mean(values, axis=-1, keepdims=True)
    center = values - mean
    return mean, jnp.sum(center * center, axis=-1, keepdims=True)


def pack_moments(values):
    mean, square = moments(values)
    count = values.shape[0]
    lane = lax.broadcasted_iota(jnp.int32, (count, LANES), 1)
    both = jnp.where(lane == 0, mean, jnp.where(lane == 1, square, 0.0))
    if count < LANES:
        both = jnp.concatenate([both, jnp.zeros((LANES - count, LANES), jnp.float32)], axis=0)
    return both.T[:8]


def unpack_moments(packed, count):
    whole = jnp.concatenate([packed, jnp.zeros((LANES - 8, LANES), jnp.float32)], axis=0).T
    return whole[:count, 0:1], whole[:count, 1:2]


def window_kernel(
    n, nb,
    keep_ref, step_ref, lat_ref, table_ref, ui_ref, do_ref, uo_ref, di_ref, uw, dw,
    out_ref,
    ad_ref, rows_all, mod_mine, gates, mod_all, stat_all, low_all, back_all, ad_all, sums_in, sums_out,
    normed, act, hid, own, stat_mine, low_mine, back_mine,
    up_buf, down_buf,
    up_sem, down_sem,
    rows_s, rows_r, mod_s, mod_r, stat_s, stat_r, low_s, low_r, back_s, back_r, ad_s, ad_r, sum_s, sum_r, left_s,
):
    me = lax.axis_index(T_NAME)
    mb = lax.axis_index(B_NAME)
    count, width = lat_ref.shape
    units = uo_ref.shape[1]
    part = ad_ref.shape[1]
    up_slots = up_buf.shape[0]
    lane_rows = width // LANES
    keep = keep_ref[0]
    f32, bf16 = jnp.float32, jnp.bfloat16

    def up_slot(level, block):
        return lax.rem(level * n + block, up_slots)

    def up_copy(level, block):
        rows = pl.ds(pl.multiple_of(block * width, LANES), width)
        return pltpu.make_async_copy(uw.at[level, rows, :], up_buf.at[up_slot(level, block)], up_sem.at[level * n + block])

    def down_copy(level, step):
        block = lax.rem(me + 1 + step, n)
        columns = pl.ds(pl.multiple_of(block * width, LANES), width)
        return pltpu.make_async_copy(dw.at[level, :, columns], down_buf.at[step], down_sem.at[level * n + step])

    for step in range(n):
        up_copy(0, lax.rem(me + step, n)).start()
    for step in range(n):
        down_copy(0, step).start()
    for step in range(up_slots - n):
        up_copy(1, step).start()

    sent = []

    def send(src, dst, s, r, where):
        copy = pltpu.make_async_remote_copy(
            src_ref=src, dst_ref=dst, send_sem=s, recv_sem=r,
            device_id=where, device_id_type=pl.DeviceIdType.MESH)
        copy.start()
        sent.append(copy)

    def arrive(buf, r):
        pltpu.make_async_remote_copy(
            src_ref=buf, dst_ref=buf, send_sem=r, recv_sem=r,
            device_id={T_NAME: lax.rem(me + 1, n)}, device_id_type=pl.DeviceIdType.MESH).wait_recv()

    def relay(kind, hop, right):
        block, target = (me - hop, me + 1) if right else (me + hop, me - 1)
        return pltpu.make_async_remote_copy(
            src_ref=rows_all.at[kind, block], dst_ref=rows_all.at[kind, block],
            send_sem=rows_s.at[kind, block], recv_sem=rows_r.at[kind, block],
            device_id={T_NAME: target}, device_id_type=pl.DeviceIdType.MESH)

    def comes(hop, right):
        return me >= hop if right else me + hop < n

    def goes(hop, right):
        return jnp.logical_and(me >= hop, me + 1 < n) if right else jnp.logical_and(me + hop < n, me > 0)

    def own_rows(kind):
        @pl.when(me + 1 < n)
        def _():
            relay(kind, 0, True).start()

        @pl.when(me > 0)
        def _():
            pltpu.make_async_remote_copy(
                src_ref=rows_all.at[kind, me], dst_ref=rows_all.at[kind, me],
                send_sem=left_s.at[kind], recv_sem=rows_r.at[kind, me],
                device_id={T_NAME: me - 1}, device_id_type=pl.DeviceIdType.MESH).start()

    def sent_rows(kind):
        @pl.when(me + 1 < n)
        def _():
            relay(kind, 0, True).wait_send()

        @pl.when(me > 0)
        def _():
            pltpu.make_async_remote_copy(
                src_ref=rows_all.at[kind, me], dst_ref=rows_all.at[kind, me],
                send_sem=left_s.at[kind], recv_sem=rows_r.at[kind, me],
                device_id={T_NAME: me - 1}, device_id_type=pl.DeviceIdType.MESH).wait_send()

        for hop in range(1, n):
            for right in (True, False):
                @pl.when(goes(hop, right))
                def _():
                    relay(kind, hop, right).wait_send()

    def walk(kind, use, between=None):
        use(me, True)
        for hop in range(1, n):
            for right in (True, False):
                @pl.when(comes(hop, right))
                def _():
                    block = me - hop if right else me + hop
                    arrive(rows_all.at[kind, block], rows_r.at[kind, block])

                @pl.when(goes(hop, right))
                def _():
                    relay(kind, hop, right).start()

            for right in (True, False):
                @pl.when(comes(hop, right))
                def _():
                    use(me - hop if right else me + hop, False)

            if hop == 1 and between is not None:
                between()

    def to_peers(src, dst, s, r):
        for step in range(1, n):
            send(src, dst, s.at[step], r.at[me], {T_NAME: lax.rem(me + step, n)})

    def from_peers(buf, r):
        for step in range(1, n):
            block = lax.rem(me + n - step, n)
            arrive(buf.at[block], r.at[block])

    rows_all[0, me] = lat_ref[...]
    stat_mine[0] = pack_moments(lat_ref[...].astype(f32))
    for level in range(2):
        chosen = lax.broadcasted_iota(jnp.int32, table_ref.shape[2:], 0) == step_ref[0]
        picked = [jnp.sum(jnp.where(chosen, table_ref[level, row].astype(f32), 0.0), axis=0, keepdims=True) for row in range(3)]
        gates[level : level + 1, :] = picked[2]
        both = [ui_ref[level].astype(f32), do_ref[level].astype(f32)]
        ad_ref[level] = jnp.concatenate(both if level == 0 else both[::-1], axis=0).T.astype(bf16)
        for row in range(2):
            for j in range(lane_rows):
                place = (2 * level + row) * lane_rows + j
                mod_mine[place : place + 1, :] = picked[row][:, j * LANES : (j + 1) * LANES]
    barrier = pltpu.get_barrier_semaphore()
    for step in range(1, n):
        pl.semaphore_signal(barrier, inc=1, device_id={T_NAME: lax.rem(me + step, n)}, device_id_type=pl.DeviceIdType.MESH)
    for step in range(1, nb):
        pl.semaphore_signal(barrier, inc=1, device_id={B_NAME: lax.rem(mb + step, nb)}, device_id_type=pl.DeviceIdType.MESH)
    pl.semaphore_wait(barrier, n - 1 + nb - 1)

    to_peers(stat_mine.at[0], stat_all.at[0, me], stat_s.at[0], stat_r.at[0])
    to_peers(mod_mine, mod_all.at[me], mod_s, mod_r)
    own_rows(0)
    spot = pl.ds(pl.multiple_of(mb * part, 16), part)
    for level in range(2):
        for step in range(1, nb):
            send(ad_ref.at[level], ad_all.at[level, spot, :], ad_s.at[level, step], ad_r.at[level, mb], {B_NAME: lax.rem(mb + step, nb)})
    mod_all[me] = mod_mine[...]
    ad_all[:, spot, :] = ad_ref[...]
    stat_all[0, me] = stat_mine[0]

    def wait_ad(level):
        for step in range(1, nb):
            other = lax.rem(mb + step, nb)
            there = pl.ds(pl.multiple_of(other * part, 16), part)
            arrive(ad_all.at[level, there, :], ad_r.at[level, other])

    def statistics(kind):
        parts = [unpack_moments(stat_all[kind, b], count) for b in range(n)]
        mean = sum(p[0] for p in parts) * (1.0 / n)
        square = sum(p[1] + width * (p[0] - mean) * (p[0] - mean) for p in parts)
        return mean, lax.rsqrt(square * (1.0 / (n * width)) + 1e-06)

    def mod_row(block, row):
        return jnp.concatenate([mod_all[block, row * lane_rows + j : row * lane_rows + j + 1, :] for j in range(lane_rows)], axis=1)

    def apply(kind, level, block, stats):
        values = rows_all[kind, block].astype(f32)
        return ((values - stats[0]) * stats[1] * (1.0 + mod_row(block, 2 * level + 1)) + mod_row(block, 2 * level)).astype(bf16)

    def up_step(slot, target, init):
        def body(start, size):
            columns = pl.ds(start, size)
            value = jnp.dot(normed[...], up_buf[slot, :, columns], preferred_element_type=f32)
            if init:
                hid[target, :, columns] = value
            else:
                hid[target, :, columns] += value

        matmul_tiles(units, 512, body)

    def add_low(target, low):
        def body(start, size):
            columns = pl.ds(start, size)
            hid[target, :, columns] += jnp.dot(low, uo_ref[:, columns], preferred_element_type=f32)

        matmul_tiles(units, 512, body)

    half = lax.broadcasted_iota(jnp.int32, (count, LANES), 1) < LANES // 2

    def low_sum(kind):
        return sum(low_all[kind, b].astype(f32) for b in range(n))

    def back_projection(level):
        value = lax.dot_general(act[...], di_ref[level], (((1,), (1,)), ((), ())), preferred_element_type=f32)
        mine = half if level == 1 else jnp.logical_not(half)
        back_mine[level] = jnp.where(mine, jnp.concatenate([value, value], axis=1), 0.0).astype(bf16)
        back_all[level, me] = back_mine[level]
        to_peers(back_mine.at[level], back_all.at[level, me], back_s.at[level], back_r.at[level])

    def down_steps(level):
        for step in range(n):
            down_copy(level, step).wait()

            def body(start, size):
                columns = pl.ds(start, size)
                value = jnp.dot(act[...], down_buf[step, :, columns], preferred_element_type=f32)
                if step < n - 1:
                    sums_out[level, step, :, columns] = value.astype(bf16)
                else:
                    own[:, columns] = value

            matmul_tiles(width, 256, body)
            if step < n - 1:
                send(sums_out.at[level, step], sums_in.at[level, me], sum_s.at[level, step], sum_r.at[level, me], {T_NAME: lax.rem(me + 1 + step, n)})
            if step == 0:
                back_projection(level)
            if level == 0:
                down_copy(1, step).start()

    def settle(level):
        from_peers(back_all.at[level], back_r.at[level])
        low = sum(back_all[level, b].astype(f32) for b in range(n)).astype(bf16)
        total = own[...] + lax.dot_general(low, ad_all[level], (((1,), (1,)), ((), ())), preferred_element_type=f32)
        from_peers(sums_in.at[level], sum_r.at[level])
        for step in range(1, n):
            total = total + sums_in[level, lax.rem(me + step, n)].astype(f32)
        return total

    from_peers(stat_all.at[0], stat_r.at[0])
    from_peers(mod_all, mod_r)
    lat_stats = statistics(0)

    def low_latent():
        wait_ad(0)
        low0 = jnp.dot(apply(0, 0, me, lat_stats), ad_all[0], preferred_element_type=f32)
        wait_ad(1)
        low1 = jnp.dot(apply(0, 1, me, lat_stats), ad_all[1], preferred_element_type=f32)
        low_mine[0] = jnp.where(half, low0, low1).astype(bf16)
        low_all[0, me] = low_mine[0]
        to_peers(low_mine.at[0], low_all.at[0, me], low_s.at[0], low_r.at[0])

    def use_latent(block, init):
        normed[...] = apply(0, 0, block, lat_stats)
        up_copy(0, block).wait()
        up_step(up_slot(0, block), 0, init)

    walk(0, use_latent, low_latent)
    for block in range(up_slots - n, n):
        up_copy(1, block).start()
    from_peers(low_all.at[0], low_r.at[0])
    add_low(0, jnp.where(half, low_sum(0), 0.0).astype(bf16))
    act[...] = jax.nn.gelu(hid[0], approximate=True).astype(bf16)
    down_steps(0)
    for block in range(n):
        normed[...] = apply(0, 1, block, lat_stats)
        up_copy(1, block).wait()
        up_step((n + block) % up_slots, 1, block == 0)
    add_low(1, jnp.where(half, 0.0, low_sum(0)).astype(bf16))
    hid[1] = jax.nn.gelu(hid[1], approximate=True)
    first = (lat_ref[...].astype(f32) + gates[0:1, :] * settle(0)).astype(bf16)
    rows_all[1, me] = first
    stat_mine[1] = pack_moments(first.astype(f32))
    to_peers(stat_mine.at[1], stat_all.at[1, me], stat_s.at[1], stat_r.at[1])
    own_rows(1)
    stat_all[1, me] = stat_mine[1]
    from_peers(stat_all.at[1], stat_r.at[1])
    stats = statistics(1)
    low = jnp.dot(apply(1, 1, me, stats), ad_all[1], preferred_element_type=f32)
    low_mine[1] = jnp.where(half, 0.0, low).astype(bf16)
    low_all[1, me] = low_mine[1]
    to_peers(low_mine.at[1], low_all.at[1, me], low_s.at[1], low_r.at[1])

    def use_first(block, init):
        normed[...] = apply(1, 1, block, stats)
        up_step(up_slot(1, block), 0, init)

    walk(1, use_first)
    from_peers(low_all.at[1], low_r.at[1])
    add_low(0, low_sum(1).astype(bf16))
    active = jax.nn.gelu(hid[0], approximate=True)
    act[...] = ((1.0 + guide_weight) * active - (guide_weight * keep) * hid[1]).astype(bf16)
    down_steps(1)
    total = settle(1)
    first_value = rows_all[1, me].astype(f32)
    start = first_value + guide_weight * keep * (first_value - lat_ref[...].astype(f32))
    out_ref[...] = (start + gates[1:2, :] * total).astype(out_ref.dtype)
    for kind in range(2):
        sent_rows(kind)
    for copy in sent:
        copy.wait_send()


def per_device_fused(n, nb, latent, mod_table, skip_layer, step_index, up_weight, down_weight, up_in, up_out, down_in, down_out):
    f32, bf16 = jnp.float32, jnp.bfloat16
    tokens = latent[0]
    count, width = tokens.shape
    units = up_weight.shape[2]
    keep = (skip_layer == 0).astype(f32)
    lane_rows = 4 * width // LANES
    uo = up_out.reshape(LANES, units)
    up_slots = n + 2
    vmem = pl.BlockSpec(memory_space=pltpu.VMEM)
    hbm = pl.BlockSpec(memory_space=pl.ANY)
    dma = pltpu.SemaphoreType.DMA
    part = up_in.shape[1]
    return pl.pallas_call(
        functools.partial(window_kernel, n, nb),
        out_shape=jax.ShapeDtypeStruct((count, width), bf16),
        in_specs=[pl.BlockSpec(memory_space=pltpu.SMEM)] * 2 + [vmem] * 6 + [hbm] * 2,
        out_specs=vmem,
        scratch_shapes=[
            pltpu.VMEM((2, part, LANES), bf16),
            pltpu.VMEM((2, n, count, width), bf16),
            pltpu.VMEM((lane_rows, LANES), f32),
            pltpu.VMEM((8, width), f32),
            pltpu.VMEM((n, lane_rows, LANES), f32),
            pltpu.VMEM((2, n, 8, LANES), f32),
            pltpu.VMEM((2, n, count, LANES), bf16),
            pltpu.VMEM((2, n, count, LANES), bf16),
            pltpu.VMEM((2, part * nb, LANES), bf16),
            pltpu.VMEM((2, n, count, width), bf16),
            pltpu.VMEM((2, n - 1, count, width), bf16),
            pltpu.VMEM((count, width), bf16),
            pltpu.VMEM((count, units), bf16),
            pltpu.VMEM((2, count, units), f32),
            pltpu.VMEM((count, width), f32),
            pltpu.VMEM((2, 8, LANES), f32),
            pltpu.VMEM((2, count, LANES), bf16),
            pltpu.VMEM((2, count, LANES), bf16),
            pltpu.VMEM((up_slots, width, units), bf16),
            pltpu.VMEM((n, units, width), bf16),
            dma((2 * n,)), dma((2 * n,)),
            dma((2, n)), dma((2, n)),
            dma((n,)), dma((n,)),
            dma((2, n)), dma((2, n)),
            dma((2, n)), dma((2, n)),
            dma((2, n)), dma((2, n)),
            dma((2, nb)), dma((2, nb)),
            dma((2, n)), dma((2, n)),
            dma((2,)),
        ],
        compiler_params=pltpu.CompilerParams(collective_id=0, has_side_effects=True, vmem_limit_bytes=63 * 2**20),
        cost_estimate=pl.CostEstimate(flops=8 * 10**9, bytes_accessed=80 * 10**6, transcendentals=400000),
    )(keep, step_index, tokens, jnp.swapaxes(mod_table, 1, 2), jnp.swapaxes(up_in, 1, 2), down_out, uo, jnp.swapaxes(down_in, 1, 2), up_weight, down_weight)[None]


def solution(mesh):
    placed = (
        P(("groups", "batch"), None, "tensor"),
        P(None, None, None, "tensor"),
        P(("groups", "batch")),
        P(("groups", "batch")),
        P(None, None, "tensor"),
        P(None, "tensor", None),
        P(None, ("tensor", "batch"), None),
        P(None, None, "tensor"),
        P(None, "tensor", None),
        P(None, None, ("tensor", "batch")),
    )
    n, nb = mesh.shape["tensor"], mesh.shape["batch"]

    def one_device(*arrays):
        latent, up_weight, up_out = arrays[0], arrays[4], arrays[7]
        count, width = latent.shape[1:]
        units, rank = up_weight.shape[2], up_out.shape[1]
        aligned = width % LANES == 0 and units % LANES == 0 and 2 * rank == LANES
        small = n * width * units * 2 <= 20 * 2**20 and n > 2 and nb > 1
        if aligned and small and count % 16 == 0 and count <= LANES:
            return per_device_fused(n, nb, *arrays)
        return per_device(*arrays)

    return jax.shard_map(
        one_device,
        mesh=mesh,
        in_specs=placed,
        out_specs=P(("groups", "batch"), None, "tensor"),
        check_vma=False,
    )
```
